128 devices in a mesh: wide: 32 (over y, x, core), narrow: 4 (over z).
Axes of the slice: x: 4, y: 4, z: 4, core: 2. Of those that a mesh axis runs over, the one named last changes fastest.
Arguments:
- cache: bfloat16 [16, 16384, 8, 128], P(None, 'wide', 'narrow'), may hold values from -24 to 24
- lengths: int32 [16], replicated, may hold values from 2 to 16384, as said below
- queries: bfloat16 [3, 2048, 4096], P(None, 'wide', 'narrow'), may hold values from -30 to 30
- new_kv: bfloat16 [3, 2048, 8, 128], P(None, 'wide', 'narrow'), may hold values from -6 to 6
- sinks: float32 [64], replicated, may hold values from 8 to 14
- residual: bfloat16 [3, 2048, 2880], P(None, ('wide', 'narrow')), may hold values from -6 to 6
- norm_gain: bfloat16 [2880], replicated, may hold values from 0.5 to 1.5
- w_out: bfloat16 [4096, 2880], P('narrow'), may hold values from -0.09375 to 0.09375
- w_router: bfloat16 [2880, 64], replicated, may hold values from -0.109375 to 0.109375
- expert_ids: int32 [3, 2048, 4], P(None, ('wide', 'narrow')), may hold values from 0 to 63, all different within a row; in each aligned block of 16 rows (0 to 15, 16 to 31, ..., all dimensions but the last counted through in order) at most 2 rows name the same one
- w_gate_up: bfloat16 [128, 2880, 2, 720], P(('wide', 'narrow')), may hold values from -0.3125 to 0.3125
- w_down: bfloat16 [128, 720, 2880], P(('wide', 'narrow')), may hold values from -0.0546875 to 0.0546875
Outputs:
- layer_out: bfloat16 [3, 2048, 2880], P(None, ('wide', 'narrow'))
The draws below stay inside these ranges and needn't reach their ends.
Inputs may be any that keep to these rules, and one draw needn't show every extreme that they name: `lengths`: the longest request uses all 16384 positions. `expert_ids`: each row names 4 different experts; within each aligned block of 16 rows of a step no expert is named more than 2 times, a bound that some block reaches.
All inputs are finite; a program needn't handle non-finite values.
Results may differ from the reference program's by a relative error of at most 0.024.
Values may be sent and summed in bfloat16 or wider, within the bound.
No kernel may reach another device: no remote copies, remote signals or barrier semaphores. Data moves between devices by JAX's collectives and lax.ppermute only.
A program may use at most 128 MiB of HBM per device.

```python
import math
import jax
import jax.numpy as jnp
import numpy as np
from jax import lax

D = 2880
HD = 64
HQ = 64
KVH = 8
EFF = 1440
TOPK = 4
STEPS = 3
ROWS_DEV = 16
LEN = 16384
EXPERTS = 64
EFF_H = 720
CAP = 2
BLOCKS = 128
ROWS = 2048
ROWS_REQ = 128
REQUESTS = 16


def draw_cache(key, part):
    key = jax.random.fold_in(key, 11)
    full_shape = (REQUESTS, LEN, KVH, 2 * HD)
    sample = jnp.clip(jax.random.normal(key, full_shape, jnp.float32), -6.0, 6.0)
    return sample.astype(jnp.bfloat16)


def draw_queries(key, part):
    key = jax.random.fold_in(key, 12)
    full_shape = (STEPS, ROWS, HQ * HD)
    sample = 2.5 * jnp.clip(jax.random.normal(key, full_shape, jnp.float32), -6.0, 6.0)
    return sample.astype(jnp.bfloat16)


def draw_lengths(key, part):
    key = jax.random.fold_in(key, 13)
    length_key, longest_key = jax.random.split(key)
    drawn_lengths = jax.random.randint(length_key, (REQUESTS,), 2, LEN + 1)
    longest = jax.random.randint(longest_key, (), 0, REQUESTS)
    return jnp.where(jnp.arange(REQUESTS) == longest, LEN, drawn_lengths).astype(jnp.int32)


def level_of(key, dims, cuts, low, largest):
    gain = 1.0
    for dim, shards_of in cuts:
        steps = jax.random.uniform(jax.random.fold_in(jax.random.fold_in(key, 6), dim), (shards_of,), jnp.float32, low / len(cuts), largest / len(cuts))
        gain = gain * jnp.repeat(jnp.exp(steps), dims[dim] // shards_of).reshape((-1,) + (1,) * (len(dims) - 1 - dim))
    return gain


def routed_block(own_key, own, number, rows, count, top, bound, lean):
    sequence = jax.random.permutation(own_key, count)
    crowded, usual = shares(count, rows * top, bound, lean, True), shares(count, rows * top, bound, lean, False)
    places = jnp.arange(count)

    def named(sizes, rotation):
        used = int((sizes > 0).sum())
        fixed = max(1, used // 4)
        moved = fixed + (places - fixed + rotation * (used - fixed)) % max(1, count - fixed)
        return jnp.zeros((count,), jnp.int32).at[sequence[jnp.where(places < fixed, places, moved)]].set(jnp.asarray(sizes, jnp.int32))

    sizes = jnp.where(number % 4 == 0, named(crowded, number // 4), named(usual, number - number // 4 - 1))
    mixed = jax.random.permutation(jax.random.fold_in(own, 3), count)
    giver, sink = mixed[0:count // 2 * 2:2], mixed[1:count // 2 * 2:2]
    room = jnp.minimum(sizes[giver] - 1, bound - sizes[sink]) // 2
    room = jnp.where((giver == sequence[0]) | (sink == sequence[0]) | (sizes[sink] == 0), 0, jnp.maximum(room, 0))
    moved = jax.random.randint(jax.random.fold_in(own, 4), (count // 2,), 0, 1 << 20) % (room + 1)
    sizes = sizes.at[giver].add(-moved).at[sink].add(moved)
    items = jnp.searchsorted(jnp.cumsum(sizes), jnp.arange(rows * top), side="right").astype(jnp.int32)
    table = items.reshape(top, rows).T
    table = table[jax.random.permutation(jax.random.fold_in(own, 1), rows)]
    rotation = jax.random.randint(jax.random.fold_in(own, 2), (rows, 1), 0, top)
    return jnp.take_along_axis(table, (jnp.arange(top)[None, :] + rotation) % top, axis=1)


def shares(amount, total, reach, slope, full):
    loads = [(1 << 20) // math.isqrt(rank ** slope) + 1 for rank in range(1, amount + 1)]
    largest = reach if full else min(reach, max(-(-total // amount), total * loads[0] // sum(loads)))
    least = 1 if total - largest >= amount - 1 else 0
    holding, spare = [largest] + [least] * (amount - 1), total - largest - least * (amount - 1)
    while spare > 0:
        candidates = [i for i in range(1, amount) if holding[i] < largest] or [i for i in range(1, amount) if holding[i] < reach]
        mass, budget = sum([loads[i] for i in candidates]), spare
        for i in candidates:
            extra = min(reach - holding[i], max(1, budget * loads[i] // mass), spare)
            holding[i] = holding[i] + extra
            spare = spare - extra
    return np.array(holding)


def gaussian(rng, shape, deviation, reach, shards=(), kind=jnp.bfloat16):
    drawn = jax.random.normal(rng, shape, jnp.float32) * deviation
    if len(shards) > 0:
        drawn = level_of(rng, shape, shards, -0.22, 0.18) * drawn
    return jnp.clip(drawn, min=-reach, max=reach).astype(kind)


def setup_inputs(seed: int = 0) -> dict:
    seeds = jax.random.split(jax.random.key(seed), 13)
    cache = draw_cache(jax.random.fold_in(seeds[12], 71), 0)
    lengths = draw_lengths(jax.random.fold_in(seeds[12], 71), 0)
    queries = draw_queries(jax.random.fold_in(seeds[12], 71), 0)
    new_kv = gaussian(seeds[3], (STEPS, ROWS, KVH, 2 * HD), 1.0, 6.0, ((1, 32), (2, 4)))
    sinks = jnp.clip(jax.random.uniform(seeds[4], (HQ,), jnp.float32, 8.0, 14.0), 8.0, 14.0)
    residual = gaussian(seeds[5], (STEPS, ROWS, D), 1.0, 6.0, ((1, 128),))
    norm_gain = jnp.clip(1.0 + 0.1 * jax.random.normal(seeds[6], (D,), jnp.float32), 0.5, 1.5).astype(jnp.bfloat16)
    w_out = gaussian(seeds[7], (HQ * HD, D), (HQ * HD) ** -0.5, 0.09375, ((0, 4),))
    w_router = gaussian(seeds[8], (D, EXPERTS), D ** -0.5, 0.109375)
    expert_ids_keys = jax.random.split(jax.random.fold_in(seeds[9], 1), STEPS * ROWS // ROWS_DEV)
    expert_ids_turns = jax.random.permutation(jax.random.fold_in(seeds[9], 3), STEPS * ROWS // ROWS_DEV)
    expert_ids = jax.vmap(lambda own, number: routed_block(jax.random.fold_in(seeds[9], 2), own, number, ROWS_DEV, EXPERTS, TOPK, CAP, 2))(expert_ids_keys, expert_ids_turns).reshape((STEPS, ROWS, TOPK))
    w_gate_up = gaussian(seeds[10], (2 * EXPERTS, D, 2, EFF_H), (D // 9) ** -0.5, 0.3125, ((0, 128),))
    w_down = gaussian(seeds[11], (2 * EXPERTS, EFF_H, D), (9 * EFF) ** -0.5, 0.0546875, ((0, 128),))
    return {"cache": cache, "lengths": lengths, "queries": queries, "new_kv": new_kv, "sinks": sinks, "residual": residual, "norm_gain": norm_gain, "w_out": w_out, "w_router": w_router, "expert_ids": expert_ids, "w_gate_up": w_gate_up, "w_down": w_down}


def reference(cache, lengths, queries, new_kv, sinks, residual, norm_gain, w_out, w_router, expert_ids, w_gate_up, w_down):
    groups = HQ // KVH
    score_scale = 1.0 / math.sqrt(HD)
    sink_grid = sinks.astype(jnp.float32).reshape(KVH, groups)
    outputs = []
    for step_index in range(STEPS):
        query_all = queries[step_index].reshape(REQUESTS, ROWS_REQ, KVH, groups, HD)
        recent_all = new_kv[:step_index + 1].reshape(step_index + 1, REQUESTS, ROWS_REQ, KVH, 2 * HD)
        recent_all = jnp.transpose(recent_all, (1, 0, 2, 3, 4)).reshape(REQUESTS, (step_index + 1) * ROWS_REQ, KVH, 2 * HD)
        recent_offset = (jnp.arange(step_index + 1, dtype=jnp.int32)[:, None] * ROWS_REQ + jnp.arange(ROWS_REQ, dtype=jnp.int32)[None, :]).reshape(-1)
        query_offset = step_index * ROWS_REQ + jnp.arange(ROWS_REQ, dtype=jnp.int32)

        def attend(inputs):
            query_rows, cache_rows, recent_rows, cache_length = inputs
            joined = jnp.concatenate([cache_rows, recent_rows], axis=0).astype(jnp.float32)
            key_rows = joined[:, :, :HD]
            value_rows = joined[:, :, HD:]
            cache_ok = jnp.arange(LEN, dtype=jnp.int32) < cache_length
            allowed = jnp.concatenate([jnp.broadcast_to(cache_ok[None, :], (ROWS_REQ, LEN)), recent_offset[None, :] <= query_offset[:, None]], axis=1)
            allow_mask = allowed[:, None, None, :]
            scores = jnp.einsum('rhge,khe->rhgk', query_rows.astype(jnp.float32), key_rows) * score_scale
            masked = jnp.where(allow_mask, scores, -1e+30)
            row_peak = jnp.maximum(lax.optimization_barrier(jnp.max(masked, axis=-1)), sink_grid[None, :, :])
            weights = jnp.where(allow_mask, jnp.exp(masked - row_peak[..., None]), 0.0)
            denominator = lax.optimization_barrier(jnp.sum(weights, axis=-1)) + jnp.exp(sink_grid[None, :, :] - row_peak)
            rounded = lax.optimization_barrier(weights.astype(jnp.bfloat16))
            numerator = jnp.einsum('rhgk,khe->rhge', rounded.astype(jnp.float32), value_rows)
            return (numerator / denominator[..., None]).astype(jnp.bfloat16)
        attended = lax.map(attend, (query_all, cache, recent_all, lengths)).reshape(ROWS, HQ * HD)
        hidden = residual[step_index].astype(jnp.float32) + jnp.dot(attended, w_out, preferred_element_type=jnp.float32)
        normed = (hidden * lax.rsqrt(lax.optimization_barrier(jnp.mean(hidden * hidden, axis=-1, keepdims=True)) + 1e-05) * norm_gain.astype(jnp.float32)).astype(jnp.bfloat16)
        logits = jnp.dot(normed, w_router, preferred_element_type=jnp.float32)
        chosen_ids = expert_ids[step_index]
        picked = (chosen_ids[:, :, None] == jnp.arange(EXPERTS, dtype=jnp.int32)[None, None, :]).astype(jnp.float32)
        chosen = lax.optimization_barrier(jnp.sum(picked * logits[:, None, :], axis=-1))
        gate_weights = jnp.exp(chosen)
        gate_weights = gate_weights / lax.optimization_barrier(jnp.sum(gate_weights, axis=-1, keepdims=True))
        flat_picks = picked.reshape(BLOCKS, ROWS_DEV * TOPK, EXPERTS)
        before = jnp.cumsum(flat_picks, axis=1) - flat_picks
        slot_rank = lax.optimization_barrier(jnp.sum(flat_picks * before, axis=-1)).astype(jnp.int32)
        slot_index = chosen_ids.reshape(BLOCKS, ROWS_DEV * TOPK) * CAP + slot_rank
        placement = (slot_index[:, :, None] == jnp.arange(EXPERTS * CAP, dtype=jnp.int32)[None, None, :]).astype(jnp.float32)
        placement = placement.reshape(BLOCKS, ROWS_DEV, TOPK, EXPERTS * CAP)
        chooser = lax.optimization_barrier(jnp.sum(placement, axis=2))
        blender = lax.optimization_barrier(jnp.sum(placement * gate_weights.reshape(BLOCKS, ROWS_DEV, TOPK)[:, :, :, None], axis=2))
        sent = jnp.einsum('brs,brc->bsc', chooser, normed.reshape(BLOCKS, ROWS_DEV, D).astype(jnp.float32)).astype(jnp.bfloat16)
        buffers = jnp.transpose(sent.reshape(BLOCKS, EXPERTS, CAP, D), (1, 0, 2, 3)).reshape(EXPERTS, BLOCKS * CAP, D)

        def expert(inputs):
            rows_in, gate_up, down_proj = inputs
            summed = jnp.zeros((BLOCKS * CAP, D), jnp.float32)
            for half_index in range(2):
                projected = jnp.dot(rows_in, gate_up[half_index].reshape(D, 2 * EFF_H), preferred_element_type=jnp.float32)
                gate_part = jnp.minimum(projected[:, :EFF_H], 7.0)
                up_part = jnp.clip(projected[:, EFF_H:], -7.0, 7.0)
                activation = (gate_part * jax.nn.sigmoid(1.702 * gate_part) * (up_part + 1.0)).astype(jnp.bfloat16)
                summed = summed + jnp.dot(activation, down_proj[half_index], preferred_element_type=jnp.float32)
            return summed
        expert_out = lax.map(expert, (buffers, w_gate_up.reshape(EXPERTS, 2, D, 2, EFF_H), w_down.reshape(EXPERTS, 2, EFF_H, D)))
        expert_out = jnp.transpose(expert_out.reshape(EXPERTS, BLOCKS, CAP, D), (1, 0, 2, 3)).reshape(BLOCKS, EXPERTS * CAP, D)
        combined = jnp.einsum('brs,bsc->brc', blender, expert_out, precision=lax.Precision.HIGHEST).reshape(ROWS, D)
        outputs.append((hidden + combined).astype(jnp.bfloat16))
    return jnp.stack(outputs)
```

```python
import functools

import jax
import jax.numpy as jnp
from jax import lax
from jax.experimental import pallas as pl
from jax.experimental.pallas import tpu as pltpu
from jax.sharding import Mesh, PartitionSpec as P

GROUPS = ((0, 1), (2,))
WIDE = ("chip", "core")
ALL = ("chip", "core", "z")
BF16 = jnp.bfloat16
F32 = jnp.float32
HEAD = 64
LANES = 128
NEG = -1e30
LIMIT = 1e30


def partner(block):
    return lax.ppermute(block, "core", [(0, 1), (1, 0)])


def from_ahead(block, distance):
    count = lax.axis_size("z")
    return lax.ppermute(block, "z", [(i, (i - distance) % count) for i in range(count)])


def swap_shards(block):
    depth = lax.axis_size("z")
    route = []
    for z in range(0, depth, 2):
        route += [(depth + z, z + 1), (z + 1, depth + z)]
    return lax.ppermute(block, ("core", "z"), route)


def tie(*arrays):
    return lax.optimization_barrier(arrays)


def round_up(size, unit):
    return -(-size // unit) * unit


def exchange(block, axis):
    return lax.all_to_all(block, axis, split_axis=0, concat_axis=0, tiled=True)


def lane_ids(shape):
    return lax.broadcasted_iota(jnp.int32, shape, len(shape) - 1)


def valid_rows(length, span, core):
    return (length // (2 * span)) * span + jnp.clip(length % (2 * span) - core * span, 0, span)


def fill_queries(q_ref, qs_ref, rows, groups):
    lane = lane_ids((rows, LANES))
    extra = jnp.where(lane == HEAD, 1.0, 0.0)
    for pair in range(groups // 2):
        both = q_ref[:, pair * LANES : (pair + 1) * LANES].astype(F32) * 0.125
        for side in range(2):
            group = 2 * pair + side
            part = both if side == 0 else pltpu.roll(both, HEAD, 1)
            qs_ref[group * rows : (group + 1) * rows, :] = jnp.where(
                lane < HEAD, part, extra
            ).astype(BF16)


def key_value_rows(block, first, valid):
    shape = block.shape
    lane = lane_ids(shape)
    position = lax.broadcasted_iota(jnp.int32, shape, 0) + first
    bias = jnp.where(position < valid, 0.0, NEG).astype(BF16)
    keys = jnp.where(lane == HEAD, bias, block)
    values = jnp.where(lane < HEAD, jnp.ones_like(block), block)
    return keys, values


def score(query_rows, keys):
    return lax.dot_general(query_rows, keys, (((1,), (1,)), ((), ())), preferred_element_type=F32)


def add_chunk(qs_ref, kv_ref, acc_ref, valid, total_rows, query_span, key_span):
    def key_block(index, carry):
        first = pl.multiple_of(index * key_span, key_span)
        keys, values = key_value_rows(kv_ref[pl.ds(first, key_span), :], first, valid)

        def query_block(number, inner):
            at = pl.ds(pl.multiple_of(number * query_span, query_span), query_span)
            weights = jnp.exp(score(qs_ref[at, :], keys)).astype(BF16)
            acc_ref[at, :] += jnp.dot(weights, values, preferred_element_type=F32)
            return inner

        return lax.fori_loop(0, total_rows // query_span, query_block, carry)

    lax.fori_loop(0, (valid + key_span - 1) // key_span, key_block, 0)


def safe_update(scores, values, at, acc_ref, peak_ref):
    old = peak_ref[at, :]
    new = jnp.maximum(old, jnp.max(scores, axis=1, keepdims=True))
    weights = jnp.exp(scores - new[:, :1]).astype(BF16)
    acc_ref[at, :] = acc_ref[at, :] * jnp.exp(old - new) + jnp.dot(
        weights, values, preferred_element_type=F32
    )
    peak_ref[at, :] = new


def first_kernel(span, groups, query_span, key_span, at_ref, q_ref, kv_ref, acc_ref, qs_ref):
    rows = q_ref.shape[0]
    fill_queries(q_ref, qs_ref, rows, groups)
    acc_ref[...] = jnp.zeros_like(acc_ref)
    valid = valid_rows(at_ref[0], span, at_ref[1])
    add_chunk(qs_ref, kv_ref, acc_ref, valid, rows * groups, query_span, key_span)


def last_kernel(
    span,
    groups,
    first_row,
    query_span,
    key_span,
    at_ref,
    sink_ref,
    q_ref,
    recent_ref,
    kv_near_ref,
    kv_far_ref,
    acc_in_ref,
    out_ref,
    acc_ref,
    qs_ref,
    peak_ref,
):
    rows = q_ref.shape[0]
    recents = recent_ref.shape[0]
    total = rows * groups
    fill_queries(q_ref, qs_ref, rows, groups)
    recent_keys, recent_values = key_value_rows(recent_ref[...], 0, recents)
    row_id = lax.broadcasted_iota(jnp.int32, (rows, recents), 0) + first_row
    causal = lane_ids((rows, recents)) <= row_id

    def recent_scores(group):
        at = pl.ds(group * rows, rows)
        return jnp.where(causal, score(qs_ref[at, :], recent_keys), NEG)

    for group in range(groups):
        at = pl.ds(group * rows, rows)
        weights = jnp.exp(recent_scores(group)).astype(BF16)
        gained = jnp.dot(weights, recent_values, preferred_element_type=F32)
        acc_ref[at, :] = acc_in_ref[at, :] + gained
    near = valid_rows(at_ref[0], span, at_ref[1])
    far = valid_rows(at_ref[0], span, 1 - at_ref[1])
    add_chunk(qs_ref, kv_far_ref, acc_ref, far, total, query_span, key_span)
    lane = lane_ids((rows, LANES))

    def finish(shifted):
        for pair in range(groups // 2):
            halves = []
            for side in range(2):
                group = 2 * pair + side
                at = pl.ds(group * rows, rows)
                sink = jnp.full((rows, LANES), sink_ref[group], F32)
                own = jnp.exp(sink - peak_ref[at, :]) if shifted else jnp.exp(sink)
                value = acc_ref[at, :]
                if side == 0:
                    halves.append(pltpu.roll(value, HEAD, 1) / (value + own))
                else:
                    halves.append(value / (pltpu.roll(value, HEAD, 1) + own))
            out_ref[:, pair * LANES : (pair + 1) * LANES] = jnp.where(
                lane < HEAD, halves[0], halves[1]
            ).astype(BF16)

    acc_lane = lane_ids((total, LANES))
    weight_sums = jnp.where(acc_lane < HEAD, acc_ref[...], 0.0)
    fits = jnp.max(jnp.where(weight_sums < LIMIT, 0.0, 1.0)) == 0.0

    @pl.when(fits)
    def plain():
        finish(False)

    @pl.when(jnp.logical_not(fits))
    def careful():
        acc_ref[...] = jnp.zeros_like(acc_ref)
        for group in range(groups):
            at = pl.ds(group * rows, rows)
            peak_ref[at, :] = jnp.full((rows, LANES), sink_ref[group], F32)
            safe_update(recent_scores(group), recent_values, at, acc_ref, peak_ref)
        block = 256
        for kv_ref, limit in ((kv_near_ref, near), (kv_far_ref, far)):

            def key_block(index, carry, kv_ref=kv_ref, limit=limit):
                first = pl.multiple_of(index * block, block)
                keys, values = key_value_rows(kv_ref[pl.ds(first, block), :], first, limit)

                def query_block(number, inner):
                    at = pl.ds(pl.multiple_of(number * block, block), block)
                    safe_update(score(qs_ref[at, :], keys), values, at, acc_ref, peak_ref)
                    return inner

                return lax.fori_loop(0, total // block, query_block, carry)

            lax.fori_loop(0, (limit + block - 1) // block, key_block, 0)
        finish(True)


SMEM_SPEC = pl.BlockSpec(memory_space=pltpu.SMEM)
VMEM_SPEC = pl.BlockSpec(memory_space=pltpu.VMEM)
ATTEND = pltpu.CompilerParams(vmem_limit_bytes=30 * 2**20)
EXPERT = pltpu.CompilerParams(vmem_limit_bytes=40 * 2**20)
SMALL = pltpu.CompilerParams(vmem_limit_bytes=16 * 2**20)


def attention_cost(rows, groups, keys):
    return pl.CostEstimate(
        flops=8 * rows * groups * keys * LANES,
        bytes_accessed=keys * LANES * 2,
        transcendentals=rows * groups * keys,
    )


def attend_first(place, q, kv, span, groups):
    rows = q.shape[0]
    total = rows * groups
    return pl.pallas_call(
        functools.partial(first_kernel, span, groups, 1024, 2048),
        out_shape=jax.ShapeDtypeStruct((total, LANES), F32),
        in_specs=[SMEM_SPEC, VMEM_SPEC, VMEM_SPEC],
        out_specs=VMEM_SPEC,
        scratch_shapes=[pltpu.VMEM((total, LANES), BF16)],
        compiler_params=ATTEND,
        cost_estimate=attention_cost(rows, groups, kv.shape[0]),
        name="attend_first",
    )(place, q, kv)


def attend_last(place, sink, q, recent, near, far, acc, span, groups, first_row):
    rows, width = q.shape
    total = rows * groups
    return pl.pallas_call(
        functools.partial(last_kernel, span, groups, first_row, 1024, 2048),
        out_shape=jax.ShapeDtypeStruct((rows, width), BF16),
        in_specs=[SMEM_SPEC, SMEM_SPEC] + [VMEM_SPEC] * 5,
        out_specs=VMEM_SPEC,
        scratch_shapes=[
            pltpu.VMEM((total, LANES), F32),
            pltpu.VMEM((total, LANES), BF16),
            pltpu.VMEM((total, LANES), F32),
        ],
        compiler_params=ATTEND,
        cost_estimate=attention_cost(rows, groups, far.shape[0]),
        name="attend_last",
    )(place, sink, q, recent, near, far, acc)


def split_kernel(side_ref, rows_ref, near_ref, far_ref):
    tile = 256
    half = tile // 2
    row = lax.broadcasted_iota(jnp.int32, (tile, tile), 0)
    column = lax.broadcasted_iota(jnp.int32, (tile, tile), 1)
    side = jnp.where(row < half, side_ref[0], 1 - side_ref[0])
    source = 2 * (row % half) + side
    chooser = jnp.where(column == source, 1.0, 0.0).astype(BF16)
    for index in range(rows_ref.shape[0] // tile):
        block = rows_ref[index * tile : (index + 1) * tile, :]
        chosen = jnp.dot(chooser, block, preferred_element_type=F32).astype(BF16)
        near_ref[index * half : (index + 1) * half, :] = chosen[:half]
        far_ref[index * half : (index + 1) * half, :] = chosen[half:]


def split_heads(side, cache):
    requests, span, kv_local, packed = cache.shape
    rows = requests * span
    tile = rows // 8
    near, far = pl.pallas_call(
        split_kernel,
        grid=(8,),
        out_shape=(jax.ShapeDtypeStruct((rows, packed), BF16),) * 2,
        in_specs=[SMEM_SPEC, pl.BlockSpec((kv_local * tile, packed), lambda i: (i, 0))],
        out_specs=(pl.BlockSpec((tile, packed), lambda i: (i, 0)),) * 2,
        compiler_params=SMALL,
        name="split_heads",
    )(side.astype(jnp.int32)[None], cache.reshape(rows * kv_local, packed))
    shape = (requests, span, packed)
    return near.reshape(shape), far.reshape(shape)


def pack_kernel(slot_ref, rows_ref, out_ref):
    rows = rows_ref.shape[0]
    tile = 128
    for first in range(0, out_ref.shape[0], tile):
        place = lax.broadcasted_iota(jnp.int32, (tile, rows), 0) + first
        hit = slot_ref[0:1, :] == place
        for k in range(1, slot_ref.shape[0]):
            hit = jnp.logical_or(hit, slot_ref[k : k + 1, :] == place)
        chooser = jnp.where(hit, 1.0, 0.0).astype(BF16)
        out_ref[first : first + tile, :] = jnp.dot(
            chooser, rows_ref[...], preferred_element_type=F32
        ).astype(BF16)


def pack_rows(slot, rows, slots):
    return pl.pallas_call(
        pack_kernel,
        out_shape=jax.ShapeDtypeStruct((slots, rows.shape[1]), BF16),
        in_specs=[VMEM_SPEC] * 2,
        out_specs=VMEM_SPEC,
        compiler_params=SMALL,
        cost_estimate=pl.CostEstimate(
            flops=2 * slots * rows.size, bytes_accessed=4 * slots * rows.shape[1], transcendentals=0
        ),
        name="pack_rows",
    )(slot, rows)


def expert_kernel(own_ref, other_ref, gate_up_ref, down_ref, own_out_ref, other_out_ref):
    tile = 256
    width = down_ref.shape[1]
    for rows_ref, out_ref in ((own_ref, own_out_ref), (other_ref, other_out_ref)):

        def step(index, carry, rows_ref=rows_ref, out_ref=out_ref):
            at = pl.ds(pl.multiple_of(index * tile, tile), tile)
            rows = rows_ref[at, :width]
            gate_part = jnp.minimum(jnp.dot(rows, gate_up_ref[0], preferred_element_type=F32), 7.0)
            up_part = jnp.clip(
                jnp.dot(rows, gate_up_ref[1], preferred_element_type=F32), -7.0, 7.0
            )
            activation = gate_part * jax.nn.sigmoid(1.702 * gate_part) * (up_part + 1.0)
            result = jnp.dot(activation.astype(BF16), down_ref[...], preferred_element_type=F32)
            out_ref[at, :width] = result.astype(BF16)
            out_ref[at, width:] = jnp.zeros((tile, out_ref.shape[1] - width), BF16)
            return carry

        lax.fori_loop(0, rows_ref.shape[0] // tile, step, 0)


def expert_rows(own, other, gate_up, down):
    return pl.pallas_call(
        expert_kernel,
        out_shape=(jax.ShapeDtypeStruct(own.shape, BF16),) * 2,
        in_specs=[VMEM_SPEC] * 4,
        out_specs=(VMEM_SPEC, VMEM_SPEC),
        compiler_params=EXPERT,
        cost_estimate=pl.CostEstimate(
            flops=4 * own.shape[0] * (gate_up.size + down.size),
            bytes_accessed=2 * (gate_up.size + down.size + 4 * own.size),
            transcendentals=2 * own.shape[0] * down.shape[0],
        ),
        name="expert_rows",
    )(own, other, gate_up, down)


def blend_kernel(slot_ref, gate_ref, back_ref, out_ref):
    rows = slot_ref.shape[0]
    place = lane_ids((rows, back_ref.shape[0]))
    blender = jnp.zeros(place.shape, F32)
    for k in range(slot_ref.shape[1]):
        blender += jnp.where(slot_ref[:, k : k + 1] == place, gate_ref[:, k : k + 1], 0.0)
    high = blender.astype(BF16)
    low = (blender - high.astype(F32)).astype(BF16)
    both = jnp.concatenate([high, low], axis=0)
    mixed = jnp.dot(both, back_ref[...], preferred_element_type=F32)
    out_ref[...] = mixed[:rows] + mixed[rows:]


def blend_rows(slot, gates, back):
    rows = slot.shape[0]
    return pl.pallas_call(
        blend_kernel,
        out_shape=jax.ShapeDtypeStruct((rows, back.shape[1]), F32),
        in_specs=[VMEM_SPEC] * 3,
        out_specs=VMEM_SPEC,
        compiler_params=SMALL,
        cost_estimate=pl.CostEstimate(
            flops=4 * rows * back.size, bytes_accessed=2 * back.size, transcendentals=0
        ),
        name="blend_rows",
    )(slot, gates, back)


def shards(
    cache,
    lengths,
    queries,
    new_kv,
    sinks,
    residual,
    norm_gain,
    w_out,
    w_router,
    expert_ids,
    w_gate_up,
    w_down,
):
    depth = lax.axis_size("z")
    side = lax.axis_index("core")
    z_index = lax.axis_index("z")
    request = lax.axis_index("chip")
    requests, span, kv_local, packed = cache.shape
    steps, own_rows, q_width = queries.shape
    head_width = q_width // kv_local
    groups = head_width // HEAD
    rows_req = 2 * own_rows
    rows_dev = own_rows // depth
    model_dim = residual.shape[2]
    experts = w_router.shape[1]
    top_k = expert_ids.shape[2]
    capacity = rows_dev * top_k * 2 // experts
    assigned = rows_dev * top_k
    first_side = side == 0

    near_out, far_out = split_heads(side, cache)
    far_out = partner(far_out)
    near = exchange(near_out, "chip").reshape(requests * span, packed)
    far = exchange(far_out, "chip").reshape(requests * span, packed)

    local = jnp.concatenate(
        [queries.reshape(steps, own_rows, kv_local, head_width), new_kv], axis=3
    )
    keep = jnp.where(first_side, local[:, :, 0], local[:, :, 1])
    got = partner(jnp.where(first_side, local[:, :, 1], local[:, :, 0]))
    joined = jnp.concatenate(
        [jnp.where(first_side, keep, got), jnp.where(first_side, got, keep)], axis=1
    )
    q_all = joined[:, :, :head_width]
    recent = joined[:, :, head_width:].reshape(steps * rows_req, packed)
    place = jnp.concatenate(
        [lax.dynamic_slice_in_dim(lengths, request, 1, 0), side.astype(jnp.int32)[None]]
    )
    sink = lax.dynamic_slice_in_dim(sinks, (z_index * kv_local + side) * groups, groups, 0)

    gain_wide = norm_gain.astype(F32)
    swapped = side != z_index % 2
    far_gate_up = swap_shards(w_gate_up)
    far_down = swap_shards(w_down)
    near, near_gate_up = tie(near, jnp.transpose(w_gate_up[0], (1, 0, 2)))
    padded = round_up(model_dim, LANES)
    ids = expert_ids.reshape(steps, assigned)
    earlier = jnp.arange(assigned)[:, None] > jnp.arange(assigned)[None, :]
    same = ids[..., :, None] == ids[..., None, :]
    rank = jnp.sum((same & earlier).astype(jnp.int32), axis=-1)
    stride = round_up(steps * capacity, 8)
    kind = ids % 4
    target = (ids // 4) * depth + 2 * (kind % 2) + kind // 2
    step_ids = jnp.arange(steps, dtype=jnp.int32)[:, None]
    slot = (target * stride + step_ids * capacity + rank).reshape(steps * rows_dev, top_k)
    ids = ids.reshape(steps * rows_dev, top_k)
    slots = experts * stride
    expert_range = jnp.arange(experts, dtype=jnp.int32)

    def span_of(group, array, axis=0):
        return lax.slice_in_dim(array, group[0], group[-1] + 1, axis=axis)

    def queries_of(group):
        return span_of(group, q_all).reshape(len(group) * rows_req, head_width)

    def finish(group, q, acc):
        return attend_last(
            place, sink, q, recent, near, far, acc, span, groups, group[0] * rows_req
        )

    def project(group, out):
        count = len(group)
        out = out.reshape(count, 2, own_rows, head_width)
        mine = jnp.where(first_side, out[:, 0], out[:, 1])
        theirs = partner(jnp.where(first_side, out[:, 1], out[:, 0]))
        attended = jnp.concatenate(
            [jnp.where(first_side, mine, theirs), jnp.where(first_side, theirs, mine)], axis=2
        )
        attended = jnp.transpose(
            attended.reshape(count, depth, rows_dev, q_width), (1, 0, 2, 3)
        ).reshape(depth * count * rows_dev, q_width)
        part = jnp.dot(attended, w_out, preferred_element_type=F32).astype(BF16)
        return part.reshape(depth, count * rows_dev, model_dim)

    def spread(parts):
        pieces = [lax.dynamic_index_in_dim(parts, z_index, 0, keepdims=False)]
        for distance in range(1, depth):
            piece = lax.dynamic_index_in_dim(
                parts, (z_index - distance) % depth, 0, keepdims=False
            )
            pieces.append(from_ahead(piece, distance))
        return pieces

    def residual_sum(group, pieces):
        base = span_of(group, residual).reshape(len(group) * rows_dev, model_dim)
        return base.astype(F32) + sum(piece.astype(F32) for piece in pieces)

    def normalize(hidden):
        normed = (
            hidden * lax.rsqrt(jnp.mean(hidden * hidden, axis=-1, keepdims=True) + 1e-05) * gain_wide
        ).astype(BF16)
        return jnp.pad(normed, ((0, 0), (0, padded - model_dim)))

    def gates_of(ids, rows):
        logits = jnp.dot(rows[:, :model_dim], w_router, preferred_element_type=F32)
        picked = ids[..., None] == expert_range
        chosen = jnp.sum(jnp.where(picked, logits[:, None, :], 0.0), axis=-1)
        gates = jnp.exp(chosen)
        return gates / jnp.sum(gates, axis=-1, keepdims=True)

    early, late = GROUPS
    q_early, q_late = queries_of(early), queries_of(late)
    acc_early = attend_first(place, q_early, near, span, groups)
    acc_early, q_late = tie(acc_early, q_late)
    acc_late = attend_first(place, q_late, near, span, groups)
    acc_late, acc_early = tie(acc_late, acc_early)
    parts_early = project(early, finish(early, q_early, acc_early))
    parts_early, acc_late = tie(parts_early, acc_late)
    pieces_early = spread(parts_early)
    out_late = finish(late, q_late, acc_late)
    parts_late = project(late, out_late)
    *pieces_early, parts_late = tie(*pieces_early, parts_late)
    pieces = pieces_early + spread(parts_late)
    hidden = jnp.concatenate(
        [residual_sum(early, pieces[:depth]), residual_sum(late, pieces[depth:])]
    )
    rows = normalize(hidden)
    sent = pack_rows(jnp.transpose(slot), rows, slots)
    sent, far_gate_up, far_down, rows = tie(sent, far_gate_up, far_down, rows)
    arrived = exchange(sent.reshape(experts, stride, padded), ("chip", "z"))
    far_gate_up = jnp.transpose(far_gate_up[0], (1, 0, 2))
    gate_up = jnp.where(swapped, far_gate_up, near_gate_up)
    down = jnp.where(swapped, far_down, w_down)[0]
    gates = gates_of(ids, rows)
    arrived, gate_up, down, gates = tie(arrived, gate_up, down, gates)
    arrived = arrived.reshape(slots, padded)
    own, other = expert_rows(arrived, partner(arrived), gate_up, down)
    done = (own.astype(F32) + partner(other).astype(F32)).astype(BF16)
    returned = exchange(done.reshape(experts, stride, padded), ("chip", "z"))
    mixed = blend_rows(slot, gates, returned.reshape(slots, padded))
    out = (hidden + mixed[:, :model_dim]).astype(BF16)
    return out.reshape(steps, rows_dev, model_dim)


def solution(mesh):
    wide = mesh.shape["wide"]
    fine = Mesh(mesh.devices.reshape(wide // 2, 2, mesh.shape["narrow"]), ALL)
    return jax.shard_map(
        shards,
        mesh=fine,
        in_specs=(
            P(None, WIDE, "z", None),
            P(),
            P(None, WIDE, "z"),
            P(None, WIDE, "z", None),
            P(),
            P(None, ALL, None),
            P(),
            P("z", None),
            P(),
            P(None, ALL, None),
            P(ALL, None, None, None),
            P(ALL, None, None),
        ),
        out_specs=P(None, ALL, None),
        check_vma=False,
    )
```

```python
import functools

import jax
import jax.numpy as jnp
from jax import lax
from jax.experimental import pallas as pl
from jax.experimental.pallas import tpu as pltpu
from jax.sharding import Mesh, PartitionSpec as P

GROUPS = ((0, 1), (2,))
WIDE = ("chip", "core")
ALL = ("chip", "core", "z")
BF16 = jnp.bfloat16
F32 = jnp.float32
HEAD = 64
LANES = 128
NEG = -1e30
LIMIT = 1e30


def partner(block):
    return lax.ppermute(block, "core", [(0, 1), (1, 0)])


def from_ahead(block, distance):
    count = lax.axis_size("z")
    return lax.ppermute(block, "z", [(i, (i - distance) % count) for i in range(count)])


def swap_shards(block):
    depth = lax.axis_size("z")
    route = []
    for z in range(0, depth, 2):
        route += [(depth + z, z + 1), (z + 1, depth + z)]
    return lax.ppermute(block, ("core", "z"), route)


def tie(*arrays):
    return lax.optimization_barrier(arrays)


def round_up(size, unit):
    return -(-size // unit) * unit


def exchange(block, axis):
    return lax.all_to_all(block, axis, split_axis=0, concat_axis=0, tiled=True)


def lane_ids(shape):
    return lax.broadcasted_iota(jnp.int32, shape, len(shape) - 1)


def valid_rows(length, span, core):
    return (length // (2 * span)) * span + jnp.clip(length % (2 * span) - core * span, 0, span)


def fill_queries(q_ref, qt_ref, rows, groups):
    row = lax.broadcasted_iota(jnp.int32, (HEAD, rows), 0)
    extra = jnp.where(row == 0, 1.0, 0.0).astype(BF16)
    for pair in range(groups // 2):
        both = q_ref[:, pair * LANES : (pair + 1) * LANES].astype(F32) * 0.125
        turned = both.T.astype(BF16)
        for side in range(2):
            first = (2 * pair + side) * rows
            qt_ref[:HEAD, first : first + rows] = turned[side * HEAD : (side + 1) * HEAD]
            qt_ref[HEAD:, first : first + rows] = extra


def key_value_rows(block, first, valid):
    shape = block.shape
    lane = lane_ids(shape)
    position = lax.broadcasted_iota(jnp.int32, shape, 0) + first
    bias = jnp.where(position < valid, 0.0, NEG).astype(BF16)
    keys = jnp.where(lane == HEAD, bias, block)
    values = jnp.where(lane < HEAD, jnp.ones_like(block), block)
    return keys, values.T


def score(keys, turned_queries):
    return jnp.dot(keys, turned_queries, preferred_element_type=F32)


def add_chunk(qt_ref, kv_ref, acc_ref, valid, total_rows, query_span, key_span):
    def key_block(index, carry):
        first = pl.multiple_of(index * key_span, key_span)
        keys, values = key_value_rows(kv_ref[pl.ds(first, key_span), :], first, valid)

        def query_block(number, inner):
            at = pl.ds(pl.multiple_of(number * query_span, query_span), query_span)
            weights = jnp.exp(score(keys, qt_ref[:, at])).astype(BF16)
            acc_ref[:, at] += jnp.dot(values, weights, preferred_element_type=F32)
            return inner

        return lax.fori_loop(0, total_rows // query_span, query_block, carry)

    lax.fori_loop(0, (valid + key_span - 1) // key_span, key_block, 0)


def safe_update(scores, values, at, acc_ref, peak_ref):
    old = peak_ref[0:1, at]
    new = jnp.maximum(old, jnp.max(scores, axis=0, keepdims=True))
    weights = jnp.exp(scores - new).astype(BF16)
    acc_ref[:, at] = acc_ref[:, at] * jnp.exp(old - new) + jnp.dot(
        values, weights, preferred_element_type=F32
    )
    peak_ref[:, at] = jnp.broadcast_to(new, (peak_ref.shape[0], new.shape[1]))


def first_kernel(span, groups, query_span, key_span, at_ref, q_ref, kv_ref, acc_ref, qt_ref):
    rows = q_ref.shape[0]
    fill_queries(q_ref, qt_ref, rows, groups)
    acc_ref[...] = jnp.zeros_like(acc_ref)
    valid = valid_rows(at_ref[0], span, at_ref[1])
    add_chunk(qt_ref, kv_ref, acc_ref, valid, rows * groups, query_span, key_span)


def last_kernel(
    span,
    groups,
    first_row,
    query_span,
    key_span,
    at_ref,
    sink_ref,
    q_ref,
    recent_ref,
    kv_near_ref,
    kv_far_ref,
    acc_in_ref,
    out_ref,
    acc_ref,
    qt_ref,
    peak_ref,
):
    rows = q_ref.shape[0]
    recents = recent_ref.shape[0]
    total = rows * groups
    fill_queries(q_ref, qt_ref, rows, groups)
    recent_keys, recent_values = key_value_rows(recent_ref[...], 0, recents)
    key_id = lax.broadcasted_iota(jnp.int32, (recents, rows), 0)
    causal = key_id <= lane_ids((recents, rows)) + first_row

    def recent_scores(group):
        return jnp.where(causal, score(recent_keys, qt_ref[:, pl.ds(group * rows, rows)]), NEG)

    for group in range(groups):
        at = pl.ds(group * rows, rows)
        weights = jnp.exp(recent_scores(group)).astype(BF16)
        acc_ref[:, at] = acc_in_ref[:, at] + jnp.dot(
            recent_values, weights, preferred_element_type=F32
        )
    near = valid_rows(at_ref[0], span, at_ref[1])
    far = valid_rows(at_ref[0], span, 1 - at_ref[1])
    add_chunk(qt_ref, kv_far_ref, acc_ref, far, total, query_span, key_span)

    def finish(shifted):
        for pair in range(groups // 2):
            halves = []
            for side in range(2):
                group = 2 * pair + side
                at = pl.ds(group * rows, rows)
                sink = jnp.full((HEAD, rows), sink_ref[group], F32)
                own = jnp.exp(sink - peak_ref[0:1, at]) if shifted else jnp.exp(sink)
                halves.append(acc_ref[HEAD:, at] / (acc_ref[:HEAD, at] + own))
            out_ref[:, pair * LANES : (pair + 1) * LANES] = (
                jnp.concatenate(halves, axis=0).T.astype(BF16)
            )

    fits = jnp.max(jnp.where(acc_ref[:HEAD, :] < LIMIT, 0.0, 1.0)) == 0.0

    @pl.when(fits)
    def plain():
        finish(False)

    @pl.when(jnp.logical_not(fits))
    def careful():
        acc_ref[...] = jnp.zeros_like(acc_ref)
        for group in range(groups):
            at = pl.ds(group * rows, rows)
            peak_ref[:, at] = jnp.full((peak_ref.shape[0], rows), sink_ref[group], F32)
            safe_update(recent_scores(group), recent_values, at, acc_ref, peak_ref)
        block = 256
        for kv_ref, limit in ((kv_near_ref, near), (kv_far_ref, far)):

            def key_block(index, carry, kv_ref=kv_ref, limit=limit):
                first = pl.multiple_of(index * block, block)
                keys, values = key_value_rows(kv_ref[pl.ds(first, block), :], first, limit)

                def query_block(number, inner):
                    at = pl.ds(pl.multiple_of(number * block, block), block)
                    safe_update(score(keys, qt_ref[:, at]), values, at, acc_ref, peak_ref)
                    return inner

                return lax.fori_loop(0, total // block, query_block, carry)

            lax.fori_loop(0, (limit + block - 1) // block, key_block, 0)
        finish(True)


SMEM_SPEC = pl.BlockSpec(memory_space=pltpu.SMEM)
VMEM_SPEC = pl.BlockSpec(memory_space=pltpu.VMEM)
ATTEND = pltpu.CompilerParams(vmem_limit_bytes=30 * 2**20)
EXPERT = pltpu.CompilerParams(vmem_limit_bytes=40 * 2**20)
SMALL = pltpu.CompilerParams(vmem_limit_bytes=16 * 2**20)


def attention_cost(rows, groups, keys):
    return pl.CostEstimate(
        flops=8 * rows * groups * keys * LANES,
        bytes_accessed=keys * LANES * 2,
        transcendentals=rows * groups * keys,
    )


def attend_first(place, q, kv, span, groups):
    rows = q.shape[0]
    total = rows * groups
    return pl.pallas_call(
        functools.partial(first_kernel, span, groups, 1024, 2048),
        out_shape=jax.ShapeDtypeStruct((LANES, total), F32),
        in_specs=[SMEM_SPEC, VMEM_SPEC, VMEM_SPEC],
        out_specs=VMEM_SPEC,
        scratch_shapes=[pltpu.VMEM((LANES, total), BF16)],
        compiler_params=ATTEND,
        cost_estimate=attention_cost(rows, groups, kv.shape[0]),
        name="attend_first",
    )(place, q, kv)


def attend_last(place, sink, q, recent, near, far, acc, span, groups, first_row):
    rows, width = q.shape
    total = rows * groups
    return pl.pallas_call(
        functools.partial(last_kernel, span, groups, first_row, 1024, 2048),
        out_shape=jax.ShapeDtypeStruct((rows, width), BF16),
        in_specs=[SMEM_SPEC, SMEM_SPEC] + [VMEM_SPEC] * 5,
        out_specs=VMEM_SPEC,
        scratch_shapes=[
            pltpu.VMEM((LANES, total), F32),
            pltpu.VMEM((LANES, total), BF16),
            pltpu.VMEM((8, total), F32),
        ],
        compiler_params=ATTEND,
        cost_estimate=attention_cost(rows, groups, far.shape[0]),
        name="attend_last",
    )(place, sink, q, recent, near, far, acc)


def split_kernel(side_ref, rows_ref, near_ref, far_ref):
    tile = 256
    half = tile // 2
    row = lax.broadcasted_iota(jnp.int32, (tile, tile), 0)
    column = lax.broadcasted_iota(jnp.int32, (tile, tile), 1)
    side = jnp.where(row < half, side_ref[0], 1 - side_ref[0])
    source = 2 * (row % half) + side
    chooser = jnp.where(column == source, 1.0, 0.0).astype(BF16)
    for index in range(rows_ref.shape[0] // tile):
        block = rows_ref[index * tile : (index + 1) * tile, :]
        chosen = jnp.dot(chooser, block, preferred_element_type=F32).astype(BF16)
        near_ref[index * half : (index + 1) * half, :] = chosen[:half]
        far_ref[index * half : (index + 1) * half, :] = chosen[half:]


def split_heads(side, cache):
    requests, span, kv_local, packed = cache.shape
    rows = requests * span
    tile = rows // 8
    near, far = pl.pallas_call(
        split_kernel,
        grid=(8,),
        out_shape=(jax.ShapeDtypeStruct((rows, packed), BF16),) * 2,
        in_specs=[SMEM_SPEC, pl.BlockSpec((kv_local * tile, packed), lambda i: (i, 0))],
        out_specs=(pl.BlockSpec((tile, packed), lambda i: (i, 0)),) * 2,
        compiler_params=SMALL,
        name="split_heads",
    )(side.astype(jnp.int32)[None], cache.reshape(rows * kv_local, packed))
    shape = (requests, span, packed)
    return near.reshape(shape), far.reshape(shape)


def pack_kernel(slot_ref, rows_ref, out_ref):
    rows = rows_ref.shape[0]
    tile = 128
    for first in range(0, out_ref.shape[0], tile):
        place = lax.broadcasted_iota(jnp.int32, (tile, rows), 0) + first
        hit = slot_ref[0:1, :] == place
        for k in range(1, slot_ref.shape[0]):
            hit = jnp.logical_or(hit, slot_ref[k : k + 1, :] == place)
        chooser = jnp.where(hit, 1.0, 0.0).astype(BF16)
        out_ref[first : first + tile, :] = jnp.dot(
            chooser, rows_ref[...], preferred_element_type=F32
        ).astype(BF16)


def pack_rows(slot, rows, slots):
    return pl.pallas_call(
        pack_kernel,
        out_shape=jax.ShapeDtypeStruct((slots, rows.shape[1]), BF16),
        in_specs=[VMEM_SPEC] * 2,
        out_specs=VMEM_SPEC,
        compiler_params=SMALL,
        cost_estimate=pl.CostEstimate(
            flops=2 * slots * rows.size, bytes_accessed=4 * slots * rows.shape[1], transcendentals=0
        ),
        name="pack_rows",
    )(slot, rows)


def expert_kernel(own_ref, other_ref, gate_up_ref, down_ref, own_out_ref, other_out_ref):
    tile = own_ref.shape[0]
    width = down_ref.shape[1]
    for rows_ref, out_ref in ((own_ref, own_out_ref), (other_ref, other_out_ref)):

        def step(index, carry, rows_ref=rows_ref, out_ref=out_ref):
            at = pl.ds(pl.multiple_of(index * tile, tile), tile)
            rows = rows_ref[at, :width]
            gate_part = jnp.minimum(jnp.dot(rows, gate_up_ref[0], preferred_element_type=F32), 7.0)
            up_part = jnp.clip(
                jnp.dot(rows, gate_up_ref[1], preferred_element_type=F32), -7.0, 7.0
            )
            activation = gate_part * jax.nn.sigmoid(1.702 * gate_part) * (up_part + 1.0)
            result = jnp.dot(activation.astype(BF16), down_ref[...], preferred_element_type=F32)
            out_ref[at, :width] = result.astype(BF16)
            out_ref[at, width:] = jnp.zeros((tile, out_ref.shape[1] - width), BF16)
            return carry

        lax.fori_loop(0, rows_ref.shape[0] // tile, step, 0)


def expert_rows(own, other, gate_up, down):
    return pl.pallas_call(
        expert_kernel,
        out_shape=(jax.ShapeDtypeStruct(own.shape, BF16),) * 2,
        in_specs=[VMEM_SPEC] * 4,
        out_specs=(VMEM_SPEC, VMEM_SPEC),
        compiler_params=EXPERT,
        cost_estimate=pl.CostEstimate(
            flops=4 * own.shape[0] * (gate_up.size + down.size),
            bytes_accessed=2 * (gate_up.size + down.size + 4 * own.size),
            transcendentals=2 * own.shape[0] * down.shape[0],
        ),
        name="expert_rows",
    )(own, other, gate_up, down)


def blend_kernel(slot_ref, gate_ref, back_ref, out_ref):
    rows = slot_ref.shape[0]
    place = lane_ids((rows, back_ref.shape[0]))
    blender = jnp.zeros(place.shape, F32)
    for k in range(slot_ref.shape[1]):
        blender += jnp.where(slot_ref[:, k : k + 1] == place, gate_ref[:, k : k + 1], 0.0)
    high = blender.astype(BF16)
    low = (blender - high.astype(F32)).astype(BF16)
    both = jnp.concatenate([high, low], axis=0)
    mixed = jnp.dot(both, back_ref[...], preferred_element_type=F32)
    out_ref[...] = mixed[:rows] + mixed[rows:]


def blend_rows(slot, gates, back):
    rows = slot.shape[0]
    return pl.pallas_call(
        blend_kernel,
        out_shape=jax.ShapeDtypeStruct((rows, back.shape[1]), F32),
        in_specs=[VMEM_SPEC] * 3,
        out_specs=VMEM_SPEC,
        compiler_params=SMALL,
        cost_estimate=pl.CostEstimate(
            flops=4 * rows * back.size, bytes_accessed=2 * back.size, transcendentals=0
        ),
        name="blend_rows",
    )(slot, gates, back)


def shards(
    cache,
    lengths,
    queries,
    new_kv,
    sinks,
    residual,
    norm_gain,
    w_out,
    w_router,
    expert_ids,
    w_gate_up,
    w_down,
):
    depth = lax.axis_size("z")
    side = lax.axis_index("core")
    z_index = lax.axis_index("z")
    request = lax.axis_index("chip")
    requests, span, kv_local, packed = cache.shape
    steps, own_rows, q_width = queries.shape
    head_width = q_width // kv_local
    groups = head_width // HEAD
    rows_req = 2 * own_rows
    rows_dev = own_rows // depth
    model_dim = residual.shape[2]
    experts = w_router.shape[1]
    top_k = expert_ids.shape[2]
    capacity = rows_dev * top_k * 2 // experts
    assigned = rows_dev * top_k
    first_side = side == 0

    near_out, far_out = split_heads(side, cache)
    far_out = partner(far_out)
    near = exchange(near_out, "chip").reshape(requests * span, packed)
    far = exchange(far_out, "chip").reshape(requests * span, packed)

    local = jnp.concatenate(
        [queries.reshape(steps, own_rows, kv_local, head_width), new_kv], axis=3
    )
    keep = jnp.where(first_side, local[:, :, 0], local[:, :, 1])
    got = partner(jnp.where(first_side, local[:, :, 1], local[:, :, 0]))
    joined = jnp.concatenate(
        [jnp.where(first_side, keep, got), jnp.where(first_side, got, keep)], axis=1
    )
    q_all = joined[:, :, :head_width]
    recent = joined[:, :, head_width:].reshape(steps * rows_req, packed)
    place = jnp.concatenate(
        [lax.dynamic_slice_in_dim(lengths, request, 1, 0), side.astype(jnp.int32)[None]]
    )
    sink = lax.dynamic_slice_in_dim(sinks, (z_index * kv_local + side) * groups, groups, 0)

    gain_wide = norm_gain.astype(F32)
    swapped = side != z_index % 2
    far_gate_up = swap_shards(w_gate_up)
    far_down = swap_shards(w_down)
    near, near_gate_up = tie(near, jnp.transpose(w_gate_up[0], (1, 0, 2)))
    padded = round_up(model_dim, LANES)
    ids = expert_ids.reshape(steps, assigned)
    earlier = jnp.arange(assigned)[:, None] > jnp.arange(assigned)[None, :]
    same = ids[..., :, None] == ids[..., None, :]
    rank = jnp.sum((same & earlier).astype(jnp.int32), axis=-1)
    stride = steps * capacity
    kind = ids % 4
    target = (ids // 4) * depth + 2 * (kind % 2) + kind // 2
    step_ids = jnp.arange(steps, dtype=jnp.int32)[:, None]
    slot = (target * stride + step_ids * capacity + rank).reshape(steps * rows_dev, top_k)
    ids = ids.reshape(steps * rows_dev, top_k)
    slots = experts * stride
    expert_range = jnp.arange(experts, dtype=jnp.int32)

    def span_of(group, array, axis=0):
        return lax.slice_in_dim(array, group[0], group[-1] + 1, axis=axis)

    def queries_of(group):
        return span_of(group, q_all).reshape(len(group) * rows_req, head_width)

    def finish(group, q, acc):
        return attend_last(
            place, sink, q, recent, near, far, acc, span, groups, group[0] * rows_req
        )

    def project(group, out):
        count = len(group)
        out = out.reshape(count, 2, own_rows, head_width)
        mine = jnp.where(first_side, out[:, 0], out[:, 1])
        theirs = partner(jnp.where(first_side, out[:, 1], out[:, 0]))
        attended = jnp.concatenate(
            [jnp.where(first_side, mine, theirs), jnp.where(first_side, theirs, mine)], axis=2
        )
        attended = jnp.transpose(
            attended.reshape(count, depth, rows_dev, q_width), (1, 0, 2, 3)
        ).reshape(depth * count * rows_dev, q_width)
        part = jnp.dot(attended, w_out, preferred_element_type=F32).astype(BF16)
        return part.reshape(depth, count * rows_dev, model_dim)

    def spread(parts):
        pieces = [lax.dynamic_index_in_dim(parts, z_index, 0, keepdims=False)]
        for distance in range(1, depth):
            piece = lax.dynamic_index_in_dim(
                parts, (z_index - distance) % depth, 0, keepdims=False
            )
            pieces.append(from_ahead(piece, distance))
        return pieces

    def residual_sum(group, pieces):
        base = span_of(group, residual).reshape(len(group) * rows_dev, model_dim)
        return base.astype(F32) + sum(piece.astype(F32) for piece in pieces)

    def normalize(hidden):
        normed = (
            hidden * lax.rsqrt(jnp.mean(hidden * hidden, axis=-1, keepdims=True) + 1e-05) * gain_wide
        ).astype(BF16)
        return jnp.pad(normed, ((0, 0), (0, padded - model_dim)))

    def gates_of(ids, rows):
        logits = jnp.dot(rows[:, :model_dim], w_router, preferred_element_type=F32)
        picked = ids[..., None] == expert_range
        chosen = jnp.sum(jnp.where(picked, logits[:, None, :], 0.0), axis=-1)
        gates = jnp.exp(chosen)
        return gates / jnp.sum(gates, axis=-1, keepdims=True)

    early, late = GROUPS
    q_early, q_late = queries_of(early), queries_of(late)
    acc_early = attend_first(place, q_early, near, span, groups)
    acc_early, q_late = tie(acc_early, q_late)
    acc_late = attend_first(place, q_late, near, span, groups)
    acc_late, acc_early = tie(acc_late, acc_early)
    parts_early = project(early, finish(early, q_early, acc_early))
    parts_early, acc_late = tie(parts_early, acc_late)
    pieces_early = spread(parts_early)
    out_late = finish(late, q_late, acc_late)
    parts_late = project(late, out_late)
    *pieces_early, parts_late = tie(*pieces_early, parts_late)
    pieces = pieces_early + spread(parts_late)
    hidden = jnp.concatenate(
        [residual_sum(early, pieces[:depth]), residual_sum(late, pieces[depth:])]
    )
    rows = normalize(hidden)
    sent = pack_rows(jnp.transpose(slot), rows, slots)
    sent, far_gate_up, far_down, rows = tie(sent, far_gate_up, far_down, rows)
    arrived = exchange(sent.reshape(experts * steps, capacity, padded), ("chip", "z"))
    far_gate_up = jnp.transpose(far_gate_up[0], (1, 0, 2))
    gate_up = jnp.where(swapped, far_gate_up, near_gate_up)
    down = jnp.where(swapped, far_down, w_down)[0]
    gates = gates_of(ids, rows)
    arrived, gate_up, down, gates = tie(arrived, gate_up, down, gates)
    arrived = arrived.reshape(slots, padded)
    own, other = expert_rows(arrived, partner(arrived), gate_up, down)
    done = (own.astype(F32) + partner(other).astype(F32)).astype(BF16)
    returned = exchange(done.reshape(experts * steps, capacity, padded), ("chip", "z"))
    mixed = blend_rows(slot, gates, returned.reshape(slots, padded))
    out = (hidden + mixed[:, :model_dim]).astype(BF16)
    return out.reshape(steps, rows_dev, model_dim)


def solution(mesh):
    wide = mesh.shape["wide"]
    fine = Mesh(mesh.devices.reshape(wide // 2, 2, mesh.shape["narrow"]), ALL)
    return jax.shard_map(
        shards,
        mesh=fine,
        in_specs=(
            P(None, WIDE, "z", None),
            P(),
            P(None, WIDE, "z"),
            P(None, WIDE, "z", None),
            P(),
            P(None, ALL, None),
            P(),
            P("z", None),
            P(),
            P(None, ALL, None),
            P(ALL, None, None, None),
            P(ALL, None, None),
        ),
        out_specs=P(None, ALL, None),
        check_vma=False,
    )
```
